32 devices in a mesh: dp: 16 (over z, y, x), mp: 2 (over core).
Axes of the slice: x: 2, y: 2, z: 4, core: 2. Of those that a mesh axis runs over, the one named last changes fastest.
Arguments:
- hidden_in: float32 [16, 128, 768], P('dp'), may hold values from -6 to 6
- lengths: int32 [16], P('dp'), may hold values from 1 to 128, as said below
- cotangent: float32 [16, 128, 768], P('dp'), may hold values from -6 to 6
- qkv_weight: bfloat16 [1, 768, 3, 768], P(None, 'dp', None, 'mp'), may hold values from -0.21875 to 0.21875
- qv_bias: bfloat16 [1, 2, 768], P(None, None, ('mp', 'dp')), may hold values from -3 to 3
- out_weight: bfloat16 [1, 768, 768], P(None, 'mp', 'dp'), may hold values from -0.875 to 0.875
- out_bias: bfloat16 [1, 768], P(None, 'dp'), may hold values from -3 to 3
- attn_gain: bfloat16 [1, 768], P(None, 'dp'), may hold values from 0.5 to 1.5
- attn_shift: bfloat16 [1, 768], P(None, 'dp'), may hold values from -3 to 3
- up_weight: bfloat16 [1, 768, 3072], P(None, 'dp', 'mp'), may hold values from -0.21875 to 0.21875
- up_bias: bfloat16 [1, 3072], P(None, ('mp', 'dp')), may hold values from -3 to 3
- down_weight: bfloat16 [1, 3072, 768], P(None, 'mp', 'dp'), may hold values from -0.109375 to 0.109375
- down_bias: bfloat16 [1, 768], P(None, 'dp'), may hold values from -3 to 3
- ffn_gain: bfloat16 [1, 768], P(None, 'dp'), may hold values from 0.5 to 1.5
- ffn_shift: bfloat16 [1, 768], P(None, 'dp'), may hold values from -3 to 3
Outputs:
- hidden_out: float32 [16, 128, 768], P('dp')
- grad_input: float32 [16, 128, 768], P('dp')
- grad_qkv_weight: float32 [1, 768, 3, 768], P(None, 'dp', None, 'mp')
- grad_qv_bias: float32 [1, 2, 768], P(None, None, ('mp', 'dp'))
- grad_out_weight: float32 [1, 768, 768], P(None, 'mp', 'dp')
- grad_out_bias: float32 [1, 768], P(None, 'dp')
- grad_attn_gain: float32 [1, 768], P(None, 'dp')
- grad_attn_shift: float32 [1, 768], P(None, 'dp')
- grad_up_weight: float32 [1, 768, 3072], P(None, 'dp', 'mp')
- grad_up_bias: float32 [1, 3072], P(None, ('mp', 'dp'))
- grad_down_weight: float32 [1, 3072, 768], P(None, 'mp', 'dp')
- grad_down_bias: float32 [1, 768], P(None, 'dp')
- grad_ffn_gain: float32 [1, 768], P(None, 'dp')
- grad_ffn_shift: float32 [1, 768], P(None, 'dp')
The draws below stay inside these ranges and needn't reach their ends.
Inputs may be any that keep to these rules, and one draw needn't show every extreme that they name: `lengths`: each sequence holds 1 to 128 tokens in its first slots, and some sequence holds exactly 128.
All inputs are finite; a program needn't handle non-finite values.
Results may differ from the reference program's by a relative error of at most 0.012.
The reference program's roundings to bfloat16 on the way count: a program that leaves them out, or rounds other values in their place, can miss the bound.
Values may be sent and summed in bfloat16 or wider, within the bound.
A program may use at most 128 MiB of HBM per device.

```python
import math
import jax
import jax.numpy as jnp
from jax import lax

D = 768
HEAD_DIM = 64
FF = 3072
LAYERS = 1
LEN = 128
SEQS = 16


def draw_lengths(key, part):
    drawn = jax.random.randint(key, (SEQS,), max(1, LEN // 16), LEN + 1, jnp.int32)
    chosen = jax.random.randint(jax.random.fold_in(key, 3), (), 0, SEQS, jnp.int32)
    return jnp.where(jnp.arange(SEQS, dtype=jnp.int32) == chosen, LEN, drawn).astype(jnp.int32)


def spiked(result, own_key, source, target, blocks, factor):
    owner, partner = [(jnp.arange(result.shape[dim]) // (result.shape[dim] // blocks)).reshape([-1 if axis == dim else 1 for axis in range(result.ndim)]) for dim in (source, target)]
    chosen = jax.random.permutation(own_key, blocks)[partner]
    strong = (owner == chosen) | (owner == (partner + blocks // 2) % blocks)
    return jnp.where(strong, factor * result, result)


def block_scale(own_key, dims, pieces, smallest, top_value):
    level, own = 1.0, jax.random.fold_in(own_key, 6)
    for axis_at, blocks in pieces:
        heights = jnp.exp(jax.random.uniform(jax.random.fold_in(own, axis_at), (blocks,), jnp.float32, smallest / len(pieces), top_value / len(pieces)))
        level = level * jnp.repeat(heights, dims[axis_at] // blocks).reshape([-1 if axis == axis_at else 1 for axis in range(len(dims))])
    return level


def noise(key, dims, width, reach, cuts=(), kind=jnp.bfloat16):
    values = jax.random.normal(key, dims, jnp.float32) * width
    if len(cuts) > 0:
        values = block_scale(key, dims, cuts, -0.22, 0.18) * values
    return jnp.clip(values, min=-reach, max=reach).astype(kind)


def heavy_noise(own_key, shape, deviation, most, pieces, heavy, held_as=jnp.bfloat16):
    result = deviation * jax.random.normal(own_key, shape, jnp.float32)
    if pieces:
        result = result * block_scale(own_key, shape, pieces, -0.22, 0.18)
    return jnp.clip(spiked(result, jax.random.fold_in(own_key, 3), *heavy), -most, most).astype(held_as)


def setup_inputs(seed: int = 0) -> dict:
    key_of = jax.random.split(jax.random.key(seed), 16)
    hidden_in = noise(key_of[0], (SEQS, LEN, D), 1.0, 6.0, ((0, 16),), jnp.float32)
    lengths = draw_lengths(jax.random.fold_in(key_of[15], 71), 0)
    cotangent = heavy_noise(key_of[2], (SEQS, LEN, D), 1.0, 6.0, ((0, 16),), (0, 2, 16, 2.0), jnp.float32)
    qkv_weight = noise(key_of[3], (LAYERS, D, 3, D), D ** -0.5, 0.21875, ((1, 16), (3, 2)))
    qv_bias = noise(key_of[4], (LAYERS, 2, D), 0.5, 3.0, ((2, 32),))
    out_weight = noise(key_of[5], (LAYERS, D, D), (D // 16) ** -0.5, 0.875, ((1, 2), (2, 16)))
    out_bias = noise(key_of[6], (LAYERS, D), 0.5, 3.0, ((1, 16),))
    attn_gain = jnp.clip(1.0 + 0.1 * jax.random.normal(key_of[7], (LAYERS, D), jnp.float32), 0.5, 1.5).astype(jnp.bfloat16)
    attn_shift = noise(key_of[8], (LAYERS, D), 0.5, 3.0, ((1, 16),))
    up_weight = noise(key_of[9], (LAYERS, D, FF), D ** -0.5, 0.21875, ((1, 16), (2, 2)))
    up_bias = noise(key_of[10], (LAYERS, FF), 0.5, 3.0, ((1, 32),))
    down_weight = noise(key_of[11], (LAYERS, FF, D), FF ** -0.5, 0.109375, ((1, 2), (2, 16)))
    down_bias = noise(key_of[12], (LAYERS, D), 0.5, 3.0, ((1, 16),))
    ffn_gain = jnp.clip(1.0 + 0.1 * jax.random.normal(key_of[13], (LAYERS, D), jnp.float32), 0.5, 1.5).astype(jnp.bfloat16)
    ffn_shift = noise(key_of[14], (LAYERS, D), 0.5, 3.0, ((1, 16),))
    return {"hidden_in": hidden_in, "lengths": lengths, "cotangent": cotangent, "qkv_weight": qkv_weight, "qv_bias": qv_bias, "out_weight": out_weight, "out_bias": out_bias, "attn_gain": attn_gain, "attn_shift": attn_shift, "up_weight": up_weight, "up_bias": up_bias, "down_weight": down_weight, "down_bias": down_bias, "ffn_gain": ffn_gain, "ffn_shift": ffn_shift}


NORM_EPS = 1e-06
MASKED = -1e+30

def normalize(residue, gain_vec, shift_vec):
    centre = residue - lax.optimization_barrier(jnp.mean(residue, axis=-1, keepdims=True))
    inverse = lax.rsqrt(lax.optimization_barrier(jnp.mean(centre * centre, axis=-1, keepdims=True)) + NORM_EPS)
    scaled = centre * inverse
    return (scaled * gain_vec + shift_vec, scaled, inverse)

def normalize_back(upstream, scaled, inverse, gain_vec):
    through = upstream * gain_vec
    d_residue = inverse * (through - lax.optimization_barrier(jnp.mean(through, axis=-1, keepdims=True)) - scaled * lax.optimization_barrier(jnp.mean(through * scaled, axis=-1, keepdims=True)))
    return (d_residue, lax.optimization_barrier(jnp.sum(upstream * scaled, axis=0)), lax.optimization_barrier(jnp.sum(upstream, axis=0)))

def gelu_exact(pre_act):
    return pre_act * 0.5 * (1.0 + lax.erf(pre_act * (1.0 / math.sqrt(2.0))))

def gelu_slope(pre_act):
    normal_cdf = 0.5 * (1.0 + lax.erf(pre_act * (1.0 / math.sqrt(2.0))))
    density = jnp.exp(-0.5 * pre_act * pre_act) * (1.0 / math.sqrt(2.0 * math.pi))
    return normal_cdf + pre_act * density

def attend_scores(queries, keys_b, keymask):
    raw = jnp.einsum('bqhe,bkhe->bhqk', queries.astype(jnp.float32), keys_b.astype(jnp.float32)) * 0.125
    return jnp.where(keymask[:, None, None, :], raw, MASKED)

def layer_forward(hidden, params, keymask):
    qkv_w, qv_b, out_w, out_b, gain_a, shift_a, up_w, up_b, down_w, down_b, gain_f, shift_f = params
    seq_count, seq_span = keymask.shape
    feat_width = hidden.shape[1]
    local_width = qkv_w.shape[2]
    heads_here = local_width // HEAD_DIM
    inputs_b = hidden.astype(jnp.bfloat16)
    projected = jnp.dot(inputs_b, qkv_w.reshape(feat_width, 3 * local_width), preferred_element_type=jnp.float32)
    projected = projected.reshape(seq_count, seq_span, 3, heads_here, HEAD_DIM)
    biases = qv_b.astype(jnp.float32).reshape(2, heads_here, HEAD_DIM)
    queries = (projected[:, :, 0] + biases[0]).astype(jnp.bfloat16)
    keys_b = projected[:, :, 1].astype(jnp.bfloat16)
    values = (projected[:, :, 2] + biases[1]).astype(jnp.bfloat16)
    scores = attend_scores(queries, keys_b, keymask)
    row_peak = lax.optimization_barrier(jnp.max(scores, axis=-1, keepdims=True))
    logsum = row_peak + jnp.log(lax.optimization_barrier(jnp.sum(jnp.exp(scores - row_peak), axis=-1, keepdims=True)))
    probs_b = jnp.exp(scores - logsum).astype(jnp.bfloat16)
    context = jnp.einsum('bhqk,bkhe->bqhe', probs_b.astype(jnp.float32), values.astype(jnp.float32))
    context = context.astype(jnp.bfloat16).reshape(seq_count * seq_span, local_width)
    attended = jnp.dot(context, out_w, preferred_element_type=jnp.float32) + out_b.astype(jnp.float32)
    mid_f, scaled_a, inverse_a = normalize(hidden + attended, gain_a.astype(jnp.float32), shift_a.astype(jnp.float32))
    mid_b = mid_f.astype(jnp.bfloat16)
    pre_act = jnp.dot(mid_b, up_w, preferred_element_type=jnp.float32) + up_b.astype(jnp.float32)
    act_b = gelu_exact(pre_act).astype(jnp.bfloat16)
    mlp_out = jnp.dot(act_b, down_w, preferred_element_type=jnp.float32) + down_b.astype(jnp.float32)
    output, scaled_f, inverse_f = normalize(mid_f + mlp_out, gain_f.astype(jnp.float32), shift_f.astype(jnp.float32))
    return (output, (inputs_b, queries, keys_b, values, logsum, context, scaled_a, inverse_a, mid_b, pre_act, act_b, scaled_f, inverse_f))

def layer_backward(upstream, params, kept_state, keymask):
    qkv_w, qv_b, out_w, out_b, gain_a, shift_a, up_w, up_b, down_w, down_b, gain_f, shift_f = params
    inputs_b, queries, keys_b, values, logsum, context, scaled_a, inverse_a, mid_b, pre_act, act_b, scaled_f, inverse_f = kept_state
    seq_count, seq_span = keymask.shape
    feat_width = upstream.shape[1]
    local_width = qkv_w.shape[2]
    heads_here = local_width // HEAD_DIM
    d_resid_f, grad_gain_f, grad_shift_f = normalize_back(upstream, scaled_f, inverse_f, gain_f.astype(jnp.float32))
    mlp_b = d_resid_f.astype(jnp.bfloat16)
    grad_down = jnp.dot(act_b.T, mlp_b, preferred_element_type=jnp.float32)
    grad_down_b = lax.optimization_barrier(jnp.sum(d_resid_f, axis=0))
    d_pre = jnp.dot(mlp_b, down_w.T, preferred_element_type=jnp.float32) * gelu_slope(pre_act)
    d_pre_b = d_pre.astype(jnp.bfloat16)
    grad_up = jnp.dot(mid_b.T, d_pre_b, preferred_element_type=jnp.float32)
    grad_up_b = lax.optimization_barrier(jnp.sum(d_pre, axis=0))
    d_mid = d_resid_f + jnp.dot(d_pre_b, up_w.T, preferred_element_type=jnp.float32)
    d_resid_a, grad_gain_a, grad_shift_a = normalize_back(d_mid, scaled_a, inverse_a, gain_a.astype(jnp.float32))
    attn_b = d_resid_a.astype(jnp.bfloat16)
    grad_out = jnp.dot(context.T, attn_b, preferred_element_type=jnp.float32)
    grad_out_b = lax.optimization_barrier(jnp.sum(d_resid_a, axis=0))
    d_context = jnp.dot(attn_b, out_w.T, preferred_element_type=jnp.float32).astype(jnp.bfloat16)
    d_context = d_context.reshape(seq_count, seq_span, heads_here, HEAD_DIM)
    scores = attend_scores(queries, keys_b, keymask)
    probs_f = jnp.exp(scores - logsum)
    probs_b = probs_f.astype(jnp.bfloat16)
    d_probs = jnp.einsum('bqhe,bkhe->bhqk', d_context.astype(jnp.float32), values.astype(jnp.float32))
    d_values = jnp.einsum('bhqk,bqhe->bkhe', probs_b.astype(jnp.float32), d_context.astype(jnp.float32))
    centred = lax.optimization_barrier(jnp.sum(probs_f * d_probs, axis=-1, keepdims=True))
    d_scores = (probs_f * (d_probs - centred) * 0.125).astype(jnp.bfloat16)
    d_queries = jnp.einsum('bhqk,bkhe->bqhe', d_scores.astype(jnp.float32), keys_b.astype(jnp.float32))
    d_keys = jnp.einsum('bhqk,bqhe->bkhe', d_scores.astype(jnp.float32), queries.astype(jnp.float32))
    grad_qv = jnp.stack([lax.optimization_barrier(jnp.sum(d_queries, axis=(0, 1))).reshape(-1), lax.optimization_barrier(jnp.sum(d_values, axis=(0, 1))).reshape(-1)])
    d_proj = jnp.stack([d_queries, d_keys, d_values], axis=2).astype(jnp.bfloat16).reshape(seq_count * seq_span, 3 * local_width)
    grad_qkv = jnp.dot(inputs_b.T, d_proj, preferred_element_type=jnp.float32).reshape(feat_width, 3, local_width)
    d_hidden = d_resid_a + jnp.dot(d_proj, qkv_w.reshape(feat_width, 3 * local_width).T, preferred_element_type=jnp.float32)
    return (d_hidden, (grad_qkv, grad_qv, grad_out, grad_out_b, grad_gain_a, grad_shift_a, grad_up, grad_up_b, grad_down, grad_down_b, grad_gain_f, grad_shift_f))

def reference(hidden_in, lengths, cotangent, qkv_weight, qv_bias, out_weight, out_bias, attn_gain, attn_shift, up_weight, up_bias, down_weight, down_bias, ffn_gain, ffn_shift):
    shards = (qkv_weight, qv_bias, out_weight, out_bias, attn_gain, attn_shift, up_weight, up_bias, down_weight, down_bias, ffn_gain, ffn_shift)
    seq_block = math.gcd(SEQS, max(1, 4096 // LEN))
    block_count = SEQS // seq_block

    def layer_params(layer_at):
        return tuple((member[layer_at] for member in shards))

    def run_block(totals, block_data):
        block_in, block_lens, block_cot = block_data
        keymask = jnp.arange(LEN)[None, :] < block_lens[:, None]
        rowmask = keymask.astype(jnp.float32).reshape(-1, 1)
        hidden = block_in.reshape(-1, D)
        kept_list = []
        for layer_at in range(LAYERS):
            hidden, kept_state = layer_forward(hidden, layer_params(layer_at), keymask)
            kept_list.append(kept_state)
        output = hidden * rowmask
        upstream = block_cot.reshape(-1, D) * rowmask
        grads_list = [None] * LAYERS
        for layer_at in reversed(range(LAYERS)):
            upstream, layer_grads = layer_backward(upstream, layer_params(layer_at), kept_list[layer_at], keymask)
            grads_list[layer_at] = layer_grads
        stacked = tuple((jnp.stack([grads_list[depth_at][member_at] for depth_at in range(LAYERS)]) for member_at in range(12)))
        totals = tuple((total + fresh for total, fresh in zip(totals, stacked)))
        return (totals, (output.reshape(seq_block, LEN, D), upstream.reshape(seq_block, LEN, D)))
    initial = tuple((jnp.zeros(member.shape, jnp.float32) for member in shards))
    block_data = (hidden_in.reshape(block_count, seq_block, LEN, D), lengths.reshape(block_count, seq_block), cotangent.reshape(block_count, seq_block, LEN, D))
    totals, (outputs, grads_in) = lax.scan(run_block, initial, block_data)
    return (outputs.reshape(SEQS, LEN, D), grads_in.reshape(SEQS, LEN, D), totals[0], totals[1], totals[2], totals[3], totals[4], totals[5], totals[6], totals[7], totals[8], totals[9], totals[10], totals[11])
```

```python
import math

import jax
import jax.numpy as jnp
from jax import lax
from jax.experimental import pallas as pl
from jax.experimental.pallas import tpu as pltpu
from jax.sharding import PartitionSpec as P

HEAD_DIM = 64


NORM_EPS = 1e-06
MASKED = -1e30


def normalize(residue, gain_vec, shift_vec):
    centre = residue - jnp.mean(residue, axis=-1, keepdims=True)
    inverse = lax.rsqrt(jnp.mean(centre * centre, axis=-1, keepdims=True) + NORM_EPS)
    scaled = centre * inverse
    return (scaled * gain_vec + shift_vec, scaled, inverse)


def normalize_back(upstream, scaled, inverse, gain_vec):
    through = upstream * gain_vec
    d_residue = inverse * (
        through
        - jnp.mean(through, axis=-1, keepdims=True)
        - scaled * jnp.mean(through * scaled, axis=-1, keepdims=True)
    )
    return (d_residue, jnp.sum(upstream * scaled, axis=0), jnp.sum(upstream, axis=0))


def gelu_exact(pre_act):
    return pre_act * 0.5 * (1.0 + lax.erf(pre_act * (1.0 / math.sqrt(2.0))))


def gelu_slope(pre_act):
    normal_cdf = 0.5 * (1.0 + lax.erf(pre_act * (1.0 / math.sqrt(2.0))))
    density = jnp.exp(-0.5 * pre_act * pre_act) * (1.0 / math.sqrt(2.0 * math.pi))
    return normal_cdf + pre_act * density


def attend_scores(queries, keys_b, keymask):
    raw = jnp.einsum("bqhe,bkhe->bhqk", queries, keys_b, preferred_element_type=jnp.float32) * 0.125
    return jnp.where(keymask[:, None, None, :], raw, MASKED)


MESH = pl.DeviceIdType.MESH
BF16 = jnp.bfloat16
F32 = jnp.float32
VMEM_LIMIT = 56 * 1024 * 1024

LINE = 4
SPAN = 16

LAST_TWO = (True, True, False, False, False)


def place_of(me):
    return me // 4, (me // 2) % 2, me % 2


def block_of(place, last, other, last_two):
    return place * 4 + (other * 2 + last if last_two else last * 2 + other)


def greet(me, place, one, two):
    barrier = pltpu.get_barrier_semaphore()
    for partner in (me + 1 - 2 * two, me + 2 - 4 * one):
        pl.semaphore_signal(barrier, inc=1, device_id={"dp": partner}, device_id_type=MESH)

    @pl.when(place > 0)
    def _():
        pl.semaphore_signal(barrier, inc=1, device_id={"dp": me - 4}, device_id_type=MESH)

    @pl.when(place < LINE - 1)
    def _():
        pl.semaphore_signal(barrier, inc=1, device_id={"dp": me + 4}, device_id_type=MESH)

    at_end = (place == 0) | (place == LINE - 1)

    @pl.when(at_end)
    def _():
        pl.semaphore_wait(barrier, 3)

    @pl.when(jnp.logical_not(at_end))
    def _():
        pl.semaphore_wait(barrier, 4)


def gather_kernel(*refs):
    count = len(LAST_TWO)
    mine, full = refs[:count], refs[count : 2 * count]
    line_send, other_send, last_send, line_recv, pair_recv = refs[2 * count :]
    me = lax.axis_index("dp")
    place, one, two = place_of(me)
    for piece in range(count):
        full[piece][me] = mine[piece][...]
    greet(me, place, one, two)

    def remote(piece, block, send_sem, recv_sem, partner):
        return pltpu.make_async_remote_copy(
            src_ref=full[piece].at[block],
            dst_ref=full[piece].at[block],
            send_sem=send_sem,
            recv_sem=recv_sem,
            device_id={"dp": partner},
            device_id_type=MESH,
        )

    def pair(piece):
        if LAST_TWO[piece]:
            return two, one, me + 1 - 2 * two, me + 2 - 4 * one
        return one, two, me + 2 - 4 * one, me + 1 - 2 * two

    def up_copy(piece, at):
        block = at * 4 + one * 2 + two
        return remote(piece, block, line_send.at[piece, 0, at], line_recv.at[piece, at], me + 4)

    def down_copy(piece, at):
        block = at * 4 + one * 2 + two
        return remote(piece, block, line_send.at[piece, 1, at], line_recv.at[piece, at], me - 4)

    def other_copy(piece, at, incoming=False):
        last, other, _, partner = pair(piece)
        block = block_of(at, last, 1 - other if incoming else other, LAST_TWO[piece])
        return remote(piece, block, other_send.at[piece, at], pair_recv.at[piece, block], partner)

    def last_copy(piece, at, far, incoming=False):
        last, other, partner, _ = pair(piece)
        block = block_of(
            at, 1 - last if incoming else last, 1 - other if far else other, LAST_TWO[piece]
        )
        return remote(
            piece, block, last_send.at[piece, int(far), at], pair_recv.at[piece, block], partner
        )

    def at_level(level, act):
        if level == 0:
            act(place, 0)
            return

        @pl.when(place - level >= 0)
        def _():
            act(place - level, -1)

        @pl.when(place + level < LINE)
        def _():
            act(place + level, 1)

    def spread(at, side):
        for piece in range(count):
            if side < 0:
                up_copy(piece, at).wait_recv()
            if side > 0:
                down_copy(piece, at).wait_recv()
            if side <= 0:
                pl.when(place < LINE - 1)(lambda: up_copy(piece, at).start())
            if side >= 0:
                pl.when(place > 0)(lambda: down_copy(piece, at).start())
            other_copy(piece, at).start()
            last_copy(piece, at, False).start()

    def pass_on(at, side):
        for piece in range(count):
            other_copy(piece, at, True).wait_recv()
            last_copy(piece, at, True).start()

    def finish(at, side):
        for piece in range(count):
            last_copy(piece, at, False, True).wait_recv()
            last_copy(piece, at, True, True).wait_recv()
            if side <= 0:
                pl.when(place < LINE - 1)(lambda: up_copy(piece, at).wait_send())
            if side >= 0:
                pl.when(place > 0)(lambda: down_copy(piece, at).wait_send())
            other_copy(piece, at).wait_send()
            last_copy(piece, at, False).wait_send()
            last_copy(piece, at, True).wait_send()

    at_level(0, spread)
    for level in range(1, LINE):
        at_level(level, spread)
        at_level(level - 1, pass_on)
    at_level(LINE - 1, pass_on)
    for level in range(LINE):
        at_level(level, finish)


def gather_pieces(pieces):
    count = len(pieces)
    return pl.pallas_call(
        gather_kernel,
        out_shape=tuple(jax.ShapeDtypeStruct((SPAN, *p.shape), p.dtype) for p in pieces),
        in_specs=[pl.BlockSpec(memory_space=pltpu.VMEM)] * count,
        out_specs=tuple([pl.BlockSpec(memory_space=pltpu.VMEM)] * count),
        scratch_shapes=[
            pltpu.SemaphoreType.DMA((count, 2, LINE)),
            pltpu.SemaphoreType.DMA((count, LINE)),
            pltpu.SemaphoreType.DMA((count, 2, LINE)),
            pltpu.SemaphoreType.DMA((count, LINE)),
            pltpu.SemaphoreType.DMA((count, SPAN)),
        ],
        compiler_params=pltpu.CompilerParams(
            collective_id=0, has_side_effects=True, vmem_limit_bytes=VMEM_LIMIT
        ),
        name="gather",
    )(*pieces)


def scatter_kernel(*refs):
    count = len(LAST_TWO)
    parts, outs = refs[:count], refs[count : 2 * count]
    scratch = refs[2 * count :]
    first_in, second_out, second_in, up_out, down_out, up_in, down_in, total = (
        scratch[i * count : (i + 1) * count] for i in range(8)
    )
    first_send, first_recv, second_send, second_recv, line_send, line_recv = scratch[8 * count :]
    me = lax.axis_index("dp")
    place, one, two = place_of(me)
    greet(me, place, one, two)
    rows = parts[0].shape[1]

    def pair(piece):
        if LAST_TWO[piece]:
            return two, one, me + 1 - 2 * two, me + 2 - 4 * one
        return one, two, me + 2 - 4 * one, me + 1 - 2 * two

    def first_copy(piece, at, far):
        bit, other, partner, _ = pair(piece)
        block = block_of(at, 1 - bit, 1 - other if far else other, LAST_TWO[piece])
        return pltpu.make_async_remote_copy(
            src_ref=parts[piece].at[block],
            dst_ref=first_in[piece].at[int(far), at],
            send_sem=first_send.at[piece, int(far), at],
            recv_sem=first_recv.at[piece, int(far), at],
            device_id={"dp": partner},
            device_id_type=MESH,
        )

    def second_copy(piece, at):
        return pltpu.make_async_remote_copy(
            src_ref=second_out[piece].at[at],
            dst_ref=second_in[piece].at[at],
            send_sem=second_send.at[piece, at],
            recv_sem=second_recv.at[piece, at],
            device_id={"dp": pair(piece)[3]},
            device_id_type=MESH,
        )

    def line_copy(piece, at, side):
        return pltpu.make_async_remote_copy(
            src_ref=(up_out if side > 0 else down_out)[piece].at[at],
            dst_ref=(up_in if side > 0 else down_in)[piece].at[at],
            send_sem=line_send.at[piece, int(side > 0), at],
            recv_sem=line_recv.at[piece, int(side > 0), at],
            device_id={"dp": me + 4 * side},
            device_id_type=MESH,
        )

    def by_rows(act):
        @pl.loop(0, rows // 16)
        def _(step):
            act(pl.ds(pl.multiple_of(step * 16, 16), 16))

    def at_level(level, act):
        if level == 0:
            act(place, 0)
            return

        @pl.when(place - level >= 0)
        def _():
            act(place - level, -1)

        @pl.when(place + level < LINE)
        def _():
            act(place + level, 1)

    def begin(at, side):
        for piece in range(count):
            first_copy(piece, at, True).start()
            first_copy(piece, at, False).start()

    def second(at, side):
        for piece in range(count):
            bit, other, _, _ = pair(piece)
            block = block_of(at, bit, 1 - other, LAST_TWO[piece])
            first_copy(piece, at, True).wait_recv()

            def add(sl, piece=piece, block=block):
                second_out[piece][at, sl] = (
                    parts[piece][block, sl].astype(F32) + first_in[piece][1, at, sl].astype(F32)
                ).astype(BF16)

            by_rows(add)
            second_copy(piece, at).start()

    def third(at, side):
        for piece in range(count):
            first_copy(piece, at, False).wait_recv()
            second_copy(piece, at).wait_recv()

            def add(sl, piece=piece):
                total[piece][sl] = (
                    parts[piece][me + (at - place) * 4, sl].astype(F32)
                    + first_in[piece][0, at, sl].astype(F32)
                    + second_in[piece][at, sl].astype(F32)
                )

            by_rows(add)
            if side >= 0:

                @pl.when(place > 0)
                def _(piece=piece):
                    line_copy(piece, at, 1).wait_recv()

                    def add(sl):
                        total[piece][sl] += up_in[piece][at, sl].astype(F32)

                    by_rows(add)

            if side <= 0:

                @pl.when(place < LINE - 1)
                def _(piece=piece):
                    line_copy(piece, at, -1).wait_recv()

                    def add(sl):
                        total[piece][sl] += down_in[piece][at, sl].astype(F32)

                    by_rows(add)

            if side == 0:

                def put(sl, piece=piece):
                    outs[piece][sl] = total[piece][sl]

            else:

                def put(sl, piece=piece):
                    (up_out if side > 0 else down_out)[piece][at, sl] = total[piece][sl].astype(BF16)

            by_rows(put)
            if side != 0:
                line_copy(piece, at, side).start()

    def finish(at, side):
        for piece in range(count):
            first_copy(piece, at, True).wait_send()
            first_copy(piece, at, False).wait_send()
            second_copy(piece, at).wait_send()
            if side != 0:
                line_copy(piece, at, side).wait_send()

    for level in reversed(range(LINE)):
        at_level(level, begin)
    at_level(LINE - 1, second)
    for level in reversed(range(LINE)):
        if level > 0:
            at_level(level - 1, second)
        at_level(level, third)
    for level in range(LINE):
        at_level(level, finish)


def scatter_pieces(parts):
    count = len(parts)
    shapes = [p.shape[1:] for p in parts]

    def scratch(lead, dtype=BF16):
        return [pltpu.VMEM((*lead, *shape), dtype) for shape in shapes]

    line = (LINE,)
    return pl.pallas_call(
        scatter_kernel,
        out_shape=tuple(jax.ShapeDtypeStruct(shape, F32) for shape in shapes),
        in_specs=[pl.BlockSpec(memory_space=pltpu.VMEM)] * count,
        out_specs=tuple([pl.BlockSpec(memory_space=pltpu.VMEM)] * count),
        scratch_shapes=[
            *scratch((2, LINE)),
            *scratch(line),
            *scratch(line),
            *scratch(line),
            *scratch(line),
            *scratch(line),
            *scratch(line),
            *scratch((), F32),
            pltpu.SemaphoreType.DMA((count, 2, LINE)),
            pltpu.SemaphoreType.DMA((count, 2, LINE)),
            pltpu.SemaphoreType.DMA((count, LINE)),
            pltpu.SemaphoreType.DMA((count, LINE)),
            pltpu.SemaphoreType.DMA((count, 2, LINE)),
            pltpu.SemaphoreType.DMA((count, 2, LINE)),
        ],
        compiler_params=pltpu.CompilerParams(
            collective_id=1, has_side_effects=True, vmem_limit_bytes=VMEM_LIMIT
        ),
        name="scatter",
    )(*parts)


def gather_all(pieces):
    if lax.axis_size("dp") == SPAN:
        return tuple(full.reshape(-1, full.shape[-1]) for full in gather_pieces(pieces))
    return tuple(lax.all_gather(piece, "dp", axis=0, tiled=True) for piece in pieces)


def scatter_all(parts):
    if lax.axis_size("dp") == SPAN:
        return scatter_pieces(tuple(p.reshape(SPAN, -1, p.shape[-1]) for p in parts))
    return tuple(
        lax.psum_scatter(p.astype(F32), "dp", scatter_dimension=0, tiled=True) for p in parts
    )


def both_cores(partial_value):
    size = lax.axis_size("mp")
    total = partial_value
    moving = partial_value
    for _ in range(size - 1):
        moving = lax.ppermute(moving, "mp", [(i, (i + 1) % size) for i in range(size)])
        total = total + moving
    return total


def dot(a, b, a_axis=1, b_axis=0):
    return lax.dot_general(a, b, (((a_axis,), (b_axis,)), ((), ())), preferred_element_type=F32)


def body(
    hidden_in, lengths, cotangent, qkv_weight, qv_bias, out_weight, out_bias, attn_gain,
    attn_shift, up_weight, up_bias, down_weight, down_bias, ffn_gain, ffn_shift,
):
    seqs, span, feat = hidden_in.shape
    span_dp = lax.axis_size("dp")
    own = feat // span_dp
    width = qkv_weight.shape[3]
    units = up_weight.shape[2]
    heads = width // HEAD_DIM
    keymask = jnp.arange(span)[None, :] < lengths[:, None]
    rowmask = keymask.astype(F32).reshape(-1, 1)
    hidden = hidden_in.reshape(-1, feat)

    vectors = jnp.concatenate(
        [
            v.reshape(own, -1)
            for v in (
                out_bias, attn_gain, attn_shift, down_bias, ffn_gain, ffn_shift, qv_bias, up_bias
            )
        ],
        axis=1,
    )
    used = vectors.shape[1]
    vectors = jnp.pad(vectors, ((0, 0), (0, 128 - used)))
    qkv_w, up_w, down_t, out_t, small = gather_all(
        (
            qkv_weight.reshape(own, 3 * width),
            up_weight[0],
            down_weight[0].T,
            out_weight[0].T,
            vectors,
        )
    )
    small = small.T.astype(F32)
    out_b, gain_a, shift_a, down_b, gain_f, shift_f = (small[i : i + 1] for i in range(6))
    qv_b = small[6].reshape(span_dp, 2, -1).transpose(1, 0, 2).reshape(2, width)
    up_b = small[7:used].T.reshape(1, units)

    inputs_b = hidden.astype(BF16)
    projected = dot(inputs_b, qkv_w).reshape(seqs, span, 3, heads, HEAD_DIM)
    biases = qv_b.reshape(2, heads, HEAD_DIM)
    queries = (projected[:, :, 0] + biases[0]).astype(BF16)
    keys_b = projected[:, :, 1].astype(BF16)
    values = (projected[:, :, 2] + biases[1]).astype(BF16)
    scores = attend_scores(queries, keys_b, keymask)
    row_peak = jnp.max(scores, axis=-1, keepdims=True)
    logsum = row_peak + jnp.log(jnp.sum(jnp.exp(scores - row_peak), axis=-1, keepdims=True))
    probs_f = jnp.exp(scores - logsum)
    probs_b = probs_f.astype(BF16)
    context = jnp.einsum("bhqk,bkhe->bqhe", probs_b, values, preferred_element_type=F32)
    context = context.astype(BF16).reshape(seqs * span, width)
    attended = both_cores(dot(context, out_t, 1, 1)) + out_b
    mid, scaled_a, inverse_a = normalize(hidden + attended, gain_a, shift_a)
    mid_b = mid.astype(BF16)
    pre_act = dot(mid_b, up_w) + up_b
    act_b = gelu_exact(pre_act).astype(BF16)
    mlp_out = both_cores(dot(act_b, down_t, 1, 1)) + down_b
    output, scaled_f, inverse_f = normalize(mid + mlp_out, gain_f, shift_f)
    hidden_out = (output * rowmask).reshape(seqs, span, feat)

    upstream = cotangent.reshape(-1, feat) * rowmask
    d_resid_f, grad_gain_f, grad_shift_f = normalize_back(upstream, scaled_f, inverse_f, gain_f)
    grad_down_b = jnp.sum(d_resid_f, axis=0)
    mlp_b = d_resid_f.astype(BF16)
    grad_down = dot(mlp_b, act_b, 0, 0)
    d_pre = dot(mlp_b, down_t) * gelu_slope(pre_act)
    d_pre_b = d_pre.astype(BF16)
    grad_up = dot(mid_b, d_pre_b, 0, 0)
    grad_up_b = jnp.sum(d_pre, axis=0)
    d_mid = d_resid_f + both_cores(dot(d_pre_b, up_w, 1, 1))
    d_resid_a, grad_gain_a, grad_shift_a = normalize_back(d_mid, scaled_a, inverse_a, gain_a)
    grad_out_b = jnp.sum(d_resid_a, axis=0)
    attn_b = d_resid_a.astype(BF16)
    grad_out = dot(attn_b, context, 0, 0)
    d_context = dot(attn_b, out_t).astype(BF16).reshape(seqs, span, heads, HEAD_DIM)
    d_probs = jnp.einsum("bqhe,bkhe->bhqk", d_context, values, preferred_element_type=F32)
    d_values = jnp.einsum("bhqk,bqhe->bkhe", probs_b, d_context, preferred_element_type=F32)
    centred = jnp.sum(probs_f * d_probs, axis=-1, keepdims=True)
    d_scores = (probs_f * (d_probs - centred) * 0.125).astype(BF16)
    d_queries = jnp.einsum("bhqk,bkhe->bqhe", d_scores, keys_b, preferred_element_type=F32)
    d_keys = jnp.einsum("bhqk,bqhe->bkhe", d_scores, queries, preferred_element_type=F32)
    grad_qv = jnp.stack(
        [jnp.sum(d_queries, axis=(0, 1)).reshape(-1), jnp.sum(d_values, axis=(0, 1)).reshape(-1)]
    )
    d_proj = (
        jnp.stack([d_queries, d_keys, d_values], axis=2)
        .astype(BF16)
        .reshape(seqs * span, 3 * width)
    )
    grad_qkv = dot(inputs_b, d_proj, 0, 0)
    grad_input = (d_resid_a + both_cores(dot(d_proj, qkv_w, 1, 1))).reshape(seqs, span, feat)

    grad_small = jnp.concatenate(
        [
            v.reshape(feat, -1)
            for v in (
                grad_out_b, grad_gain_a, grad_shift_a, grad_down_b, grad_gain_f, grad_shift_f,
                grad_qv.reshape(2, span_dp, -1).transpose(1, 0, 2), grad_up_b,
            )
        ],
        axis=1,
    )
    grad_small = jnp.pad(grad_small, ((0, 0), (0, 128 - used)))
    qkv_g, up_g, down_g, out_g, small_g = scatter_all(
        tuple(g.astype(BF16) for g in (grad_qkv, grad_up, grad_down, grad_out, grad_small))
    )
    vec = [small_g[:, i].reshape(1, own) for i in range(6)]
    return (
        hidden_out,
        grad_input,
        qkv_g.reshape(1, own, 3, width),
        small_g[:, 6].reshape(1, 2, -1),
        out_g.T[None],
        vec[0],
        vec[1],
        vec[2],
        up_g[None],
        small_g[:, 7:used].reshape(1, -1),
        down_g.T[None],
        vec[3],
        vec[4],
        vec[5],
    )


def solution(mesh):
    return jax.shard_map(
        body,
        mesh=mesh,
        in_specs=(
            P("dp", None, None),
            P("dp"),
            P("dp", None, None),
            P(None, "dp", None, "mp"),
            P(None, None, ("mp", "dp")),
            P(None, "mp", "dp"),
            P(None, "dp"),
            P(None, "dp"),
            P(None, "dp"),
            P(None, "dp", "mp"),
            P(None, ("mp", "dp")),
            P(None, "mp", "dp"),
            P(None, "dp"),
            P(None, "dp"),
            P(None, "dp"),
        ),
        out_specs=(
            P("dp", None, None),
            P("dp", None, None),
            P(None, "dp", None, "mp"),
            P(None, None, ("mp", "dp")),
            P(None, "mp", "dp"),
            P(None, "dp"),
            P(None, "dp"),
            P(None, "dp"),
            P(None, "dp", "mp"),
            P(None, ("mp", "dp")),
            P(None, "mp", "dp"),
            P(None, "dp"),
            P(None, "dp"),
            P(None, "dp"),
        ),
        check_vma=False,
    )
```

```python
import math

import jax
import jax.numpy as jnp
from jax import lax
from jax.experimental import pallas as pl
from jax.experimental.pallas import tpu as pltpu
from jax.sharding import PartitionSpec as P

HEAD_DIM = 64


NORM_EPS = 1e-06
MASKED = -1e30


def normalize(residue, gain_vec, shift_vec):
    centre = residue - jnp.mean(residue, axis=-1, keepdims=True)
    inverse = lax.rsqrt(jnp.mean(centre * centre, axis=-1, keepdims=True) + NORM_EPS)
    scaled = centre * inverse
    return (scaled * gain_vec + shift_vec, scaled, inverse)


def normalize_back(upstream, scaled, inverse, gain_vec):
    through = upstream * gain_vec
    d_residue = inverse * (
        through
        - jnp.mean(through, axis=-1, keepdims=True)
        - scaled * jnp.mean(through * scaled, axis=-1, keepdims=True)
    )
    return (d_residue, jnp.sum(upstream * scaled, axis=0), jnp.sum(upstream, axis=0))


def gelu_exact(pre_act):
    return pre_act * 0.5 * (1.0 + lax.erf(pre_act * (1.0 / math.sqrt(2.0))))


def gelu_slope(pre_act):
    normal_cdf = 0.5 * (1.0 + lax.erf(pre_act * (1.0 / math.sqrt(2.0))))
    density = jnp.exp(-0.5 * pre_act * pre_act) * (1.0 / math.sqrt(2.0 * math.pi))
    return normal_cdf + pre_act * density


def attend_scores(queries, keys_b, keymask):
    raw = jnp.einsum("bqhe,bkhe->bhqk", queries, keys_b, preferred_element_type=jnp.float32) * 0.125
    return jnp.where(keymask[:, None, None, :], raw, MASKED)


MESH = pl.DeviceIdType.MESH
BF16 = jnp.bfloat16
F32 = jnp.float32
VMEM_LIMIT = 56 * 1024 * 1024

LINE = 4
SPAN = 16

LAST_TWO = (True, True, False, False, False)


def place_of(me):
    return me // 4, (me // 2) % 2, me % 2


def block_of(place, last, other, last_two):
    return place * 4 + (other * 2 + last if last_two else last * 2 + other)


def greet(me, place, one, two):
    barrier = pltpu.get_barrier_semaphore()
    for partner in (me + 1 - 2 * two, me + 2 - 4 * one):
        pl.semaphore_signal(barrier, inc=1, device_id={"dp": partner}, device_id_type=MESH)

    @pl.when(place > 0)
    def _():
        pl.semaphore_signal(barrier, inc=1, device_id={"dp": me - 4}, device_id_type=MESH)

    @pl.when(place < LINE - 1)
    def _():
        pl.semaphore_signal(barrier, inc=1, device_id={"dp": me + 4}, device_id_type=MESH)

    at_end = (place == 0) | (place == LINE - 1)

    @pl.when(at_end)
    def _():
        pl.semaphore_wait(barrier, 3)

    @pl.when(jnp.logical_not(at_end))
    def _():
        pl.semaphore_wait(barrier, 4)


def gather_kernel(*refs):
    count = len(LAST_TWO)
    mine, full = refs[:count], refs[count : 2 * count]
    line_send, other_send, last_send, line_recv, pair_recv = refs[2 * count :]
    me = lax.axis_index("dp")
    place, one, two = place_of(me)
    for piece in range(count):
        full[piece][me] = mine[piece][...]
    greet(me, place, one, two)

    def remote(piece, block, send_sem, recv_sem, partner):
        return pltpu.make_async_remote_copy(
            src_ref=full[piece].at[block],
            dst_ref=full[piece].at[block],
            send_sem=send_sem,
            recv_sem=recv_sem,
            device_id={"dp": partner},
            device_id_type=MESH,
        )

    def pair(piece):
        if LAST_TWO[piece]:
            return two, one, me + 1 - 2 * two, me + 2 - 4 * one
        return one, two, me + 2 - 4 * one, me + 1 - 2 * two

    def up_copy(piece, at):
        block = at * 4 + one * 2 + two
        return remote(piece, block, line_send.at[piece, 0, at], line_recv.at[piece, at], me + 4)

    def down_copy(piece, at):
        block = at * 4 + one * 2 + two
        return remote(piece, block, line_send.at[piece, 1, at], line_recv.at[piece, at], me - 4)

    def other_copy(piece, at, incoming=False):
        last, other, _, partner = pair(piece)
        block = block_of(at, last, 1 - other if incoming else other, LAST_TWO[piece])
        return remote(piece, block, other_send.at[piece, at], pair_recv.at[piece, block], partner)

    def last_copy(piece, at, far, incoming=False):
        last, other, partner, _ = pair(piece)
        block = block_of(
            at, 1 - last if incoming else last, 1 - other if far else other, LAST_TWO[piece]
        )
        return remote(
            piece, block, last_send.at[piece, int(far), at], pair_recv.at[piece, block], partner
        )

    def at_level(level, act):
        if level == 0:
            act(place, 0)
            return

        @pl.when(place - level >= 0)
        def _():
            act(place - level, -1)

        @pl.when(place + level < LINE)
        def _():
            act(place + level, 1)

    def spread(at, side):
        for piece in range(count):
            if side < 0:
                up_copy(piece, at).wait_recv()
            if side > 0:
                down_copy(piece, at).wait_recv()
            if side <= 0:
                pl.when(place < LINE - 1)(lambda: up_copy(piece, at).start())
            if side >= 0:
                pl.when(place > 0)(lambda: down_copy(piece, at).start())
            other_copy(piece, at).start()
        for piece in range(count):
            last_copy(piece, at, False).start()

    def pass_on(at, side):
        for piece in range(count):
            other_copy(piece, at, True).wait_recv()
            last_copy(piece, at, True).start()

    def finish(at, side):
        for piece in range(count):
            last_copy(piece, at, False, True).wait_recv()
            last_copy(piece, at, True, True).wait_recv()
            if side <= 0:
                pl.when(place < LINE - 1)(lambda: up_copy(piece, at).wait_send())
            if side >= 0:
                pl.when(place > 0)(lambda: down_copy(piece, at).wait_send())
            other_copy(piece, at).wait_send()
            last_copy(piece, at, False).wait_send()
            last_copy(piece, at, True).wait_send()

    at_level(0, spread)
    for level in range(1, LINE):
        at_level(level, spread)
        at_level(level - 1, pass_on)
    at_level(LINE - 1, pass_on)
    for level in range(LINE):
        at_level(level, finish)


def gather_pieces(pieces):
    count = len(pieces)
    return pl.pallas_call(
        gather_kernel,
        out_shape=tuple(jax.ShapeDtypeStruct((SPAN, *p.shape), p.dtype) for p in pieces),
        in_specs=[pl.BlockSpec(memory_space=pltpu.VMEM)] * count,
        out_specs=tuple([pl.BlockSpec(memory_space=pltpu.VMEM)] * count),
        scratch_shapes=[
            pltpu.SemaphoreType.DMA((count, 2, LINE)),
            pltpu.SemaphoreType.DMA((count, LINE)),
            pltpu.SemaphoreType.DMA((count, 2, LINE)),
            pltpu.SemaphoreType.DMA((count, LINE)),
            pltpu.SemaphoreType.DMA((count, SPAN)),
        ],
        compiler_params=pltpu.CompilerParams(
            collective_id=0, has_side_effects=True, vmem_limit_bytes=VMEM_LIMIT
        ),
        name="gather",
    )(*pieces)


def scatter_kernel(*refs):
    count = len(LAST_TWO)
    parts, outs = refs[:count], refs[count : 2 * count]
    scratch = refs[2 * count :]
    first_in, second_out, second_in, up_out, down_out, up_in, down_in, total = (
        scratch[i * count : (i + 1) * count] for i in range(8)
    )
    first_send, first_recv, second_send, second_recv, line_send, line_recv = scratch[8 * count :]
    me = lax.axis_index("dp")
    place, one, two = place_of(me)
    greet(me, place, one, two)

    def pair(piece):
        if LAST_TWO[piece]:
            return two, one, me + 1 - 2 * two, me + 2 - 4 * one
        return one, two, me + 2 - 4 * one, me + 1 - 2 * two

    def first_copy(piece, at, far):
        bit, other, partner, _ = pair(piece)
        block = block_of(at, 1 - bit, 1 - other if far else other, LAST_TWO[piece])
        return pltpu.make_async_remote_copy(
            src_ref=parts[piece].at[block],
            dst_ref=first_in[piece].at[int(far), at],
            send_sem=first_send.at[piece, int(far), at],
            recv_sem=first_recv.at[piece, int(far), at],
            device_id={"dp": partner},
            device_id_type=MESH,
        )

    def second_copy(piece, at):
        return pltpu.make_async_remote_copy(
            src_ref=second_out[piece].at[at],
            dst_ref=second_in[piece].at[at],
            send_sem=second_send.at[piece, at],
            recv_sem=second_recv.at[piece, at],
            device_id={"dp": pair(piece)[3]},
            device_id_type=MESH,
        )

    def line_copy(piece, at, side):
        return pltpu.make_async_remote_copy(
            src_ref=(up_out if side > 0 else down_out)[piece].at[at],
            dst_ref=(up_in if side > 0 else down_in)[piece].at[at],
            send_sem=line_send.at[piece, int(side > 0), at],
            recv_sem=line_recv.at[piece, int(side > 0), at],
            device_id={"dp": me + 4 * side},
            device_id_type=MESH,
        )

    def by_rows(piece, act):
        @pl.loop(0, parts[piece].shape[1] // 16)
        def _(step):
            act(pl.ds(pl.multiple_of(step * 16, 16), 16))

    def at_level(level, act):
        if level == 0:
            act(place, 0)
            return

        @pl.when(place - level >= 0)
        def _():
            act(place - level, -1)

        @pl.when(place + level < LINE)
        def _():
            act(place + level, 1)

    def begin(at, side):
        for piece in range(count):
            first_copy(piece, at, True).start()
        for piece in range(count):
            first_copy(piece, at, False).start()

    def second(at, side):
        for piece in range(count):
            bit, other, _, _ = pair(piece)
            block = block_of(at, bit, 1 - other, LAST_TWO[piece])
            first_copy(piece, at, True).wait_recv()

            def add(sl, piece=piece, block=block):
                second_out[piece][at, sl] = (
                    parts[piece][block, sl].astype(F32) + first_in[piece][1, at, sl].astype(F32)
                ).astype(BF16)

            by_rows(piece, add)
            second_copy(piece, at).start()

    def third(at, side):
        for piece in range(count):
            first_copy(piece, at, False).wait_recv()
            second_copy(piece, at).wait_recv()

            def add(sl, piece=piece):
                total[piece][sl] = (
                    parts[piece][me + (at - place) * 4, sl].astype(F32)
                    + first_in[piece][0, at, sl].astype(F32)
                    + second_in[piece][at, sl].astype(F32)
                )

            by_rows(piece, add)
            if side >= 0:

                @pl.when(place > 0)
                def _(piece=piece):
                    line_copy(piece, at, 1).wait_recv()

                    def add(sl):
                        total[piece][sl] += up_in[piece][at, sl].astype(F32)

                    by_rows(piece, add)

            if side <= 0:

                @pl.when(place < LINE - 1)
                def _(piece=piece):
                    line_copy(piece, at, -1).wait_recv()

                    def add(sl):
                        total[piece][sl] += down_in[piece][at, sl].astype(F32)

                    by_rows(piece, add)

            if side == 0:

                def put(sl, piece=piece):
                    outs[piece][sl] = total[piece][sl]

            else:

                def put(sl, piece=piece):
                    (up_out if side > 0 else down_out)[piece][at, sl] = total[piece][sl].astype(BF16)

            by_rows(piece, put)
            if side != 0:
                line_copy(piece, at, side).start()

    def finish(at, side):
        for piece in range(count):
            first_copy(piece, at, True).wait_send()
            first_copy(piece, at, False).wait_send()
            second_copy(piece, at).wait_send()
            if side != 0:
                line_copy(piece, at, side).wait_send()

    for level in reversed(range(LINE)):
        at_level(level, begin)
    at_level(LINE - 1, second)
    for level in reversed(range(LINE)):
        if level > 0:
            at_level(level - 1, second)
        at_level(level, third)
    for level in range(LINE):
        at_level(level, finish)


def scatter_pieces(parts):
    count = len(parts)
    shapes = [p.shape[1:] for p in parts]

    def scratch(lead, dtype=BF16):
        return [pltpu.VMEM((*lead, *shape), dtype) for shape in shapes]

    line = (LINE,)
    return pl.pallas_call(
        scatter_kernel,
        out_shape=tuple(jax.ShapeDtypeStruct(shape, F32) for shape in shapes),
        in_specs=[pl.BlockSpec(memory_space=pltpu.VMEM)] * count,
        out_specs=tuple([pl.BlockSpec(memory_space=pltpu.VMEM)] * count),
        scratch_shapes=[
            *scratch((2, LINE)),
            *scratch(line),
            *scratch(line),
            *scratch(line),
            *scratch(line),
            *scratch(line),
            *scratch(line),
            *scratch((), F32),
            pltpu.SemaphoreType.DMA((count, 2, LINE)),
            pltpu.SemaphoreType.DMA((count, 2, LINE)),
            pltpu.SemaphoreType.DMA((count, LINE)),
            pltpu.SemaphoreType.DMA((count, LINE)),
            pltpu.SemaphoreType.DMA((count, 2, LINE)),
            pltpu.SemaphoreType.DMA((count, 2, LINE)),
        ],
        compiler_params=pltpu.CompilerParams(
            collective_id=1, has_side_effects=True, vmem_limit_bytes=VMEM_LIMIT
        ),
        name="scatter",
    )(*parts)


def gather_all(pieces):
    if lax.axis_size("dp") == SPAN:
        return tuple(full.reshape(-1, full.shape[-1]) for full in gather_pieces(pieces))
    return tuple(lax.all_gather(piece, "dp", axis=0, tiled=True) for piece in pieces)


def scatter_all(parts):
    if lax.axis_size("dp") == SPAN:
        return scatter_pieces(tuple(p.reshape(SPAN, -1, p.shape[-1]) for p in parts))
    return tuple(
        lax.psum_scatter(p.astype(F32), "dp", scatter_dimension=0, tiled=True) for p in parts
    )


def both_cores(partial_value):
    size = lax.axis_size("mp")
    total = partial_value
    moving = partial_value
    for _ in range(size - 1):
        moving = lax.ppermute(moving, "mp", [(i, (i + 1) % size) for i in range(size)])
        total = total + moving
    return total


def dot(a, b, a_axis=1, b_axis=0):
    return lax.dot_general(a, b, (((a_axis,), (b_axis,)), ((), ())), preferred_element_type=F32)


def body(
    hidden_in, lengths, cotangent, qkv_weight, qv_bias, out_weight, out_bias, attn_gain,
    attn_shift, up_weight, up_bias, down_weight, down_bias, ffn_gain, ffn_shift,
):
    seqs, span, feat = hidden_in.shape
    span_dp = lax.axis_size("dp")
    own = feat // span_dp
    width = qkv_weight.shape[3]
    units = up_weight.shape[2]
    heads = width // HEAD_DIM
    keymask = jnp.arange(span)[None, :] < lengths[:, None]
    rowmask = keymask.astype(F32).reshape(-1, 1)
    hidden = hidden_in.reshape(-1, feat)

    vectors = jnp.concatenate(
        [
            v.reshape(-1, own)
            for v in (
                out_bias, attn_gain, attn_shift, down_bias, ffn_gain, ffn_shift, qv_bias, up_bias
            )
        ],
        axis=0,
    )
    used = vectors.shape[0]
    vectors = jnp.pad(vectors, ((0, 16 - used), (0, 128 - own)))
    qkv_w, up_w, down_t, out_t, small = gather_all(
        (
            qkv_weight.reshape(own, 3 * width),
            up_weight[0],
            down_weight[0].T,
            out_weight[0].T,
            vectors,
        )
    )
    small = small.reshape(span_dp, 16, 128)[:, :used, :own].astype(F32)
    rows = small[:, :6].transpose(1, 0, 2).reshape(6, feat)
    out_b, gain_a, shift_a, down_b, gain_f, shift_f = (rows[i : i + 1] for i in range(6))
    qv_b = small[:, 6].reshape(span_dp, 2, -1).transpose(1, 0, 2).reshape(2, width)
    up_b = small[:, 7:].reshape(1, units)

    inputs_b = hidden.astype(BF16)
    projected = dot(inputs_b, qkv_w).reshape(seqs, span, 3, heads, HEAD_DIM)
    biases = qv_b.reshape(2, heads, HEAD_DIM)
    queries = (projected[:, :, 0] + biases[0]).astype(BF16)
    keys_b = projected[:, :, 1].astype(BF16)
    values = (projected[:, :, 2] + biases[1]).astype(BF16)
    scores = attend_scores(queries, keys_b, keymask)
    row_peak = jnp.max(scores, axis=-1, keepdims=True)
    logsum = row_peak + jnp.log(jnp.sum(jnp.exp(scores - row_peak), axis=-1, keepdims=True))
    probs_f = jnp.exp(scores - logsum)
    probs_b = probs_f.astype(BF16)
    context = jnp.einsum("bhqk,bkhe->bqhe", probs_b, values, preferred_element_type=F32)
    context = context.astype(BF16).reshape(seqs * span, width)
    attended = both_cores(dot(context, out_t, 1, 1)) + out_b
    mid, scaled_a, inverse_a = normalize(hidden + attended, gain_a, shift_a)
    mid_b = mid.astype(BF16)
    pre_act = dot(mid_b, up_w) + up_b
    act_b = gelu_exact(pre_act).astype(BF16)
    mlp_out = both_cores(dot(act_b, down_t, 1, 1)) + down_b
    output, scaled_f, inverse_f = normalize(mid + mlp_out, gain_f, shift_f)
    hidden_out = (output * rowmask).reshape(seqs, span, feat)

    upstream = cotangent.reshape(-1, feat) * rowmask
    d_resid_f, grad_gain_f, grad_shift_f = normalize_back(upstream, scaled_f, inverse_f, gain_f)
    grad_down_b = jnp.sum(d_resid_f, axis=0)
    mlp_b = d_resid_f.astype(BF16)
    grad_down = dot(mlp_b, act_b, 0, 0)
    d_pre = dot(mlp_b, down_t) * gelu_slope(pre_act)
    d_pre_b = d_pre.astype(BF16)
    grad_up = dot(mid_b, d_pre_b, 0, 0)
    grad_up_b = jnp.sum(d_pre, axis=0)
    d_mid = d_resid_f + both_cores(dot(d_pre_b, up_w, 1, 1))
    d_resid_a, grad_gain_a, grad_shift_a = normalize_back(d_mid, scaled_a, inverse_a, gain_a)
    grad_out_b = jnp.sum(d_resid_a, axis=0)
    attn_b = d_resid_a.astype(BF16)
    grad_out = dot(attn_b, context, 0, 0)
    d_context = dot(attn_b, out_t).astype(BF16).reshape(seqs, span, heads, HEAD_DIM)
    d_probs = jnp.einsum("bqhe,bkhe->bhqk", d_context, values, preferred_element_type=F32)
    d_values = jnp.einsum("bhqk,bqhe->bkhe", probs_b, d_context, preferred_element_type=F32)
    centred = jnp.sum(probs_f * d_probs, axis=-1, keepdims=True)
    d_scores = (probs_f * (d_probs - centred) * 0.125).astype(BF16)
    d_queries = jnp.einsum("bhqk,bkhe->bqhe", d_scores, keys_b, preferred_element_type=F32)
    d_keys = jnp.einsum("bhqk,bqhe->bkhe", d_scores, queries, preferred_element_type=F32)
    grad_qv = jnp.stack(
        [jnp.sum(d_queries, axis=(0, 1)).reshape(-1), jnp.sum(d_values, axis=(0, 1)).reshape(-1)]
    )
    d_proj = (
        jnp.stack([d_queries, d_keys, d_values], axis=2)
        .astype(BF16)
        .reshape(seqs * span, 3 * width)
    )
    grad_qkv = dot(inputs_b, d_proj, 0, 0)
    grad_input = (d_resid_a + both_cores(dot(d_proj, qkv_w, 1, 1))).reshape(seqs, span, feat)

    grad_rows = jnp.stack(
        [grad_out_b, grad_gain_a, grad_shift_a, grad_down_b, grad_gain_f, grad_shift_f]
    )
    grad_small = jnp.concatenate(
        [
            grad_rows.reshape(6, span_dp, own).transpose(1, 0, 2),
            grad_qv.reshape(2, span_dp, -1).transpose(1, 0, 2).reshape(span_dp, 1, own),
            grad_up_b.reshape(span_dp, -1, own),
        ],
        axis=1,
    )
    grad_small = jnp.pad(grad_small, ((0, 0), (0, 16 - used), (0, 128 - own))).reshape(-1, 128)
    qkv_g, up_g, down_g, out_g, small_g = scatter_all(
        tuple(g.astype(BF16) for g in (grad_qkv, grad_up, grad_down, grad_out, grad_small))
    )
    vec = [small_g[i : i + 1, :own] for i in range(6)]
    return (
        hidden_out,
        grad_input,
        qkv_g.reshape(1, own, 3, width),
        small_g[6, :own].reshape(1, 2, -1),
        out_g.T[None],
        vec[0],
        vec[1],
        vec[2],
        up_g[None],
        small_g[7:used, :own].reshape(1, -1),
        down_g.T[None],
        vec[3],
        vec[4],
        vec[5],
    )


def solution(mesh):
    return jax.shard_map(
        body,
        mesh=mesh,
        in_specs=(
            P("dp", None, None),
            P("dp"),
            P("dp", None, None),
            P(None, "dp", None, "mp"),
            P(None, None, ("mp", "dp")),
            P(None, "mp", "dp"),
            P(None, "dp"),
            P(None, "dp"),
            P(None, "dp"),
            P(None, "dp", "mp"),
            P(None, ("mp", "dp")),
            P(None, "mp", "dp"),
            P(None, "dp"),
            P(None, "dp"),
            P(None, "dp"),
        ),
        out_specs=(
            P("dp", None, None),
            P("dp", None, None),
            P(None, "dp", None, "mp"),
            P(None, None, ("mp", "dp")),
            P(None, "mp", "dp"),
            P(None, "dp"),
            P(None, "dp"),
            P(None, "dp"),
            P(None, "dp", "mp"),
            P(None, ("mp", "dp")),
            P(None, "mp", "dp"),
            P(None, "dp"),
            P(None, "dp"),
            P(None, "dp"),
        ),
        check_vma=False,
    )
```

```python
import math

import jax
import jax.numpy as jnp
from jax import lax
from jax.experimental import pallas as pl
from jax.experimental.pallas import tpu as pltpu
from jax.sharding import PartitionSpec as P

HEAD_DIM = 64


NORM_EPS = 1e-06
MASKED = -1e30


def normalize(residue, gain_vec, shift_vec):
    centre = residue - jnp.mean(residue, axis=-1, keepdims=True)
    inverse = lax.rsqrt(jnp.mean(centre * centre, axis=-1, keepdims=True) + NORM_EPS)
    scaled = centre * inverse
    return (scaled * gain_vec + shift_vec, scaled, inverse)


def normalize_back(upstream, scaled, inverse, gain_vec):
    through = upstream * gain_vec
    d_residue = inverse * (
        through
        - jnp.mean(through, axis=-1, keepdims=True)
        - scaled * jnp.mean(through * scaled, axis=-1, keepdims=True)
    )
    return (d_residue, jnp.sum(upstream * scaled, axis=0), jnp.sum(upstream, axis=0))


def gelu_exact(pre_act):
    return pre_act * 0.5 * (1.0 + lax.erf(pre_act * (1.0 / math.sqrt(2.0))))


def gelu_slope(pre_act):
    normal_cdf = 0.5 * (1.0 + lax.erf(pre_act * (1.0 / math.sqrt(2.0))))
    density = jnp.exp(-0.5 * pre_act * pre_act) * (1.0 / math.sqrt(2.0 * math.pi))
    return normal_cdf + pre_act * density


def attend_scores(queries, keys_b, keymask):
    raw = jnp.einsum("bqhe,bkhe->bhqk", queries, keys_b, preferred_element_type=jnp.float32) * 0.125
    return jnp.where(keymask[:, None, None, :], raw, MASKED)


MESH = pl.DeviceIdType.MESH
BF16 = jnp.bfloat16
F32 = jnp.float32
VMEM_LIMIT = 56 * 1024 * 1024

LINE = 4
SPAN = 16

LAST_TWO = (True, False, True, False, False, True)


def place_of(me):
    return me // 4, (me // 2) % 2, me % 2


def block_of(place, last, other, last_two):
    return place * 4 + (other * 2 + last if last_two else last * 2 + other)


def greet(me, place, one, two):
    barrier = pltpu.get_barrier_semaphore()
    for partner in (me + 1 - 2 * two, me + 2 - 4 * one):
        pl.semaphore_signal(barrier, inc=1, device_id={"dp": partner}, device_id_type=MESH)

    @pl.when(place > 0)
    def _():
        pl.semaphore_signal(barrier, inc=1, device_id={"dp": me - 4}, device_id_type=MESH)

    @pl.when(place < LINE - 1)
    def _():
        pl.semaphore_signal(barrier, inc=1, device_id={"dp": me + 4}, device_id_type=MESH)

    at_end = (place == 0) | (place == LINE - 1)

    @pl.when(at_end)
    def _():
        pl.semaphore_wait(barrier, 3)

    @pl.when(jnp.logical_not(at_end))
    def _():
        pl.semaphore_wait(barrier, 4)


def gather_kernel(*refs):
    count = len(LAST_TWO)
    mine, full = refs[:count], refs[count : 2 * count]
    line_send, other_send, last_send, line_recv, pair_recv = refs[2 * count :]
    me = lax.axis_index("dp")
    place, one, two = place_of(me)
    for piece in range(count):
        full[piece][me] = mine[piece][...]
    greet(me, place, one, two)

    def remote(piece, block, send_sem, recv_sem, partner):
        return pltpu.make_async_remote_copy(
            src_ref=full[piece].at[block],
            dst_ref=full[piece].at[block],
            send_sem=send_sem,
            recv_sem=recv_sem,
            device_id={"dp": partner},
            device_id_type=MESH,
        )

    def pair(piece):
        if LAST_TWO[piece]:
            return two, one, me + 1 - 2 * two, me + 2 - 4 * one
        return one, two, me + 2 - 4 * one, me + 1 - 2 * two

    def up_copy(piece, at):
        block = at * 4 + one * 2 + two
        return remote(piece, block, line_send.at[piece, 0, at], line_recv.at[piece, at], me + 4)

    def down_copy(piece, at):
        block = at * 4 + one * 2 + two
        return remote(piece, block, line_send.at[piece, 1, at], line_recv.at[piece, at], me - 4)

    def other_copy(piece, at, incoming=False):
        last, other, _, partner = pair(piece)
        block = block_of(at, last, 1 - other if incoming else other, LAST_TWO[piece])
        return remote(piece, block, other_send.at[piece, at], pair_recv.at[piece, block], partner)

    def last_copy(piece, at, far, incoming=False):
        last, other, partner, _ = pair(piece)
        block = block_of(
            at, 1 - last if incoming else last, 1 - other if far else other, LAST_TWO[piece]
        )
        return remote(
            piece, block, last_send.at[piece, int(far), at], pair_recv.at[piece, block], partner
        )

    def at_level(level, act):
        if level == 0:
            act(place, 0)
            return

        @pl.when(place - level >= 0)
        def _():
            act(place - level, -1)

        @pl.when(place + level < LINE)
        def _():
            act(place + level, 1)

    def spread(at, side):
        for piece in range(count):
            if side < 0:
                up_copy(piece, at).wait_recv()
            if side > 0:
                down_copy(piece, at).wait_recv()
            if side <= 0:
                pl.when(place < LINE - 1)(lambda: up_copy(piece, at).start())
            if side >= 0:
                pl.when(place > 0)(lambda: down_copy(piece, at).start())
            other_copy(piece, at).start()
        for piece in range(count):
            last_copy(piece, at, False).start()

    def pass_on(at, side):
        for piece in range(count):
            other_copy(piece, at, True).wait_recv()
            last_copy(piece, at, True).start()

    def finish(at, side):
        for piece in range(count):
            last_copy(piece, at, False, True).wait_recv()
            last_copy(piece, at, True, True).wait_recv()
            if side <= 0:
                pl.when(place < LINE - 1)(lambda: up_copy(piece, at).wait_send())
            if side >= 0:
                pl.when(place > 0)(lambda: down_copy(piece, at).wait_send())
            other_copy(piece, at).wait_send()
            last_copy(piece, at, False).wait_send()
            last_copy(piece, at, True).wait_send()

    at_level(0, spread)
    for level in range(1, LINE):
        at_level(level, spread)
        at_level(level - 1, pass_on)
    at_level(LINE - 1, pass_on)
    for level in range(LINE):
        at_level(level, finish)


def gather_pieces(pieces):
    count = len(pieces)
    return pl.pallas_call(
        gather_kernel,
        out_shape=tuple(jax.ShapeDtypeStruct((SPAN, *p.shape), p.dtype) for p in pieces),
        in_specs=[pl.BlockSpec(memory_space=pltpu.VMEM)] * count,
        out_specs=tuple([pl.BlockSpec(memory_space=pltpu.VMEM)] * count),
        scratch_shapes=[
            pltpu.SemaphoreType.DMA((count, 2, LINE)),
            pltpu.SemaphoreType.DMA((count, LINE)),
            pltpu.SemaphoreType.DMA((count, 2, LINE)),
            pltpu.SemaphoreType.DMA((count, LINE)),
            pltpu.SemaphoreType.DMA((count, SPAN)),
        ],
        compiler_params=pltpu.CompilerParams(
            collective_id=0, has_side_effects=True, vmem_limit_bytes=VMEM_LIMIT
        ),
        name="gather",
    )(*pieces)


def scatter_kernel(*refs):
    count = len(LAST_TWO)
    parts, outs = refs[:count], refs[count : 2 * count]
    scratch = refs[2 * count :]
    first_in, second_out, second_in, up_out, down_out, up_in, down_in, total = (
        scratch[i * count : (i + 1) * count] for i in range(8)
    )
    first_send, first_recv, second_send, second_recv, line_send, line_recv = scratch[8 * count :]
    me = lax.axis_index("dp")
    place, one, two = place_of(me)
    greet(me, place, one, two)

    def pair(piece):
        if LAST_TWO[piece]:
            return two, one, me + 1 - 2 * two, me + 2 - 4 * one
        return one, two, me + 2 - 4 * one, me + 1 - 2 * two

    def first_copy(piece, at, far):
        bit, other, partner, _ = pair(piece)
        block = block_of(at, 1 - bit, 1 - other if far else other, LAST_TWO[piece])
        return pltpu.make_async_remote_copy(
            src_ref=parts[piece].at[block],
            dst_ref=first_in[piece].at[int(far), at],
            send_sem=first_send.at[piece, int(far), at],
            recv_sem=first_recv.at[piece, int(far), at],
            device_id={"dp": partner},
            device_id_type=MESH,
        )

    def second_copy(piece, at):
        return pltpu.make_async_remote_copy(
            src_ref=second_out[piece].at[at],
            dst_ref=second_in[piece].at[at],
            send_sem=second_send.at[piece, at],
            recv_sem=second_recv.at[piece, at],
            device_id={"dp": pair(piece)[3]},
            device_id_type=MESH,
        )

    def line_copy(piece, at, side):
        return pltpu.make_async_remote_copy(
            src_ref=(up_out if side > 0 else down_out)[piece].at[at],
            dst_ref=(up_in if side > 0 else down_in)[piece].at[at],
            send_sem=line_send.at[piece, int(side > 0), at],
            recv_sem=line_recv.at[piece, int(side > 0), at],
            device_id={"dp": me + 4 * side},
            device_id_type=MESH,
        )

    def by_rows(piece, act):
        @pl.loop(0, parts[piece].shape[1] // 16)
        def _(step):
            act(pl.ds(pl.multiple_of(step * 16, 16), 16))

    def at_level(level, act):
        if level == 0:
            act(place, 0)
            return

        @pl.when(place - level >= 0)
        def _():
            act(place - level, -1)

        @pl.when(place + level < LINE)
        def _():
            act(place + level, 1)

    def begin(at, side):
        for piece in range(count):
            first_copy(piece, at, True).start()
        for piece in range(count):
            first_copy(piece, at, False).start()

    def second(at, side):
        for piece in range(count):
            bit, other, _, _ = pair(piece)
            block = block_of(at, bit, 1 - other, LAST_TWO[piece])
            first_copy(piece, at, True).wait_recv()

            def add(sl, piece=piece, block=block):
                second_out[piece][at, sl] = (
                    parts[piece][block, sl].astype(F32) + first_in[piece][1, at, sl].astype(F32)
                ).astype(BF16)

            by_rows(piece, add)
            second_copy(piece, at).start()

    def third(at, side):
        for piece in range(count):
            first_copy(piece, at, False).wait_recv()
            second_copy(piece, at).wait_recv()

            def add(sl, piece=piece):
                total[piece][sl] = (
                    parts[piece][me + (at - place) * 4, sl].astype(F32)
                    + first_in[piece][0, at, sl].astype(F32)
                    + second_in[piece][at, sl].astype(F32)
                )

            by_rows(piece, add)
            if side >= 0:

                @pl.when(place > 0)
                def _(piece=piece):
                    line_copy(piece, at, 1).wait_recv()

                    def add(sl):
                        total[piece][sl] += up_in[piece][at, sl].astype(F32)

                    by_rows(piece, add)

            if side <= 0:

                @pl.when(place < LINE - 1)
                def _(piece=piece):
                    line_copy(piece, at, -1).wait_recv()

                    def add(sl):
                        total[piece][sl] += down_in[piece][at, sl].astype(F32)

                    by_rows(piece, add)

            if side == 0:

                def put(sl, piece=piece):
                    outs[piece][sl] = total[piece][sl]

            else:

                def put(sl, piece=piece):
                    (up_out if side > 0 else down_out)[piece][at, sl] = total[piece][sl].astype(BF16)

            by_rows(piece, put)
            if side != 0:
                line_copy(piece, at, side).start()

    def finish(at, side):
        for piece in range(count):
            first_copy(piece, at, True).wait_send()
            first_copy(piece, at, False).wait_send()
            second_copy(piece, at).wait_send()
            if side != 0:
                line_copy(piece, at, side).wait_send()

    for level in reversed(range(LINE)):
        at_level(level, begin)
    at_level(LINE - 1, second)
    for level in reversed(range(LINE)):
        if level > 0:
            at_level(level - 1, second)
        at_level(level, third)
    for level in range(LINE):
        at_level(level, finish)


def scatter_pieces(parts):
    count = len(parts)
    shapes = [p.shape[1:] for p in parts]

    def scratch(lead, dtype=BF16):
        return [pltpu.VMEM((*lead, *shape), dtype) for shape in shapes]

    line = (LINE,)
    return pl.pallas_call(
        scatter_kernel,
        out_shape=tuple(jax.ShapeDtypeStruct(shape, F32) for shape in shapes),
        in_specs=[pl.BlockSpec(memory_space=pltpu.VMEM)] * count,
        out_specs=tuple([pl.BlockSpec(memory_space=pltpu.VMEM)] * count),
        scratch_shapes=[
            *scratch((2, LINE)),
            *scratch(line),
            *scratch(line),
            *scratch(line),
            *scratch(line),
            *scratch(line),
            *scratch(line),
            *scratch((), F32),
            pltpu.SemaphoreType.DMA((count, 2, LINE)),
            pltpu.SemaphoreType.DMA((count, 2, LINE)),
            pltpu.SemaphoreType.DMA((count, LINE)),
            pltpu.SemaphoreType.DMA((count, LINE)),
            pltpu.SemaphoreType.DMA((count, 2, LINE)),
            pltpu.SemaphoreType.DMA((count, 2, LINE)),
        ],
        compiler_params=pltpu.CompilerParams(
            collective_id=1, has_side_effects=True, vmem_limit_bytes=VMEM_LIMIT
        ),
        name="scatter",
    )(*parts)


def gather_all(pieces):
    if lax.axis_size("dp") == SPAN:
        return tuple(full.reshape(-1, full.shape[-1]) for full in gather_pieces(pieces))
    return tuple(lax.all_gather(piece, "dp", axis=0, tiled=True) for piece in pieces)


def scatter_all(parts):
    if lax.axis_size("dp") == SPAN:
        return scatter_pieces(tuple(p.reshape(SPAN, -1, p.shape[-1]) for p in parts))
    return tuple(
        lax.psum_scatter(p.astype(F32), "dp", scatter_dimension=0, tiled=True) for p in parts
    )


def both_cores(partial_value):
    size = lax.axis_size("mp")
    total = partial_value
    moving = partial_value
    for _ in range(size - 1):
        moving = lax.ppermute(moving, "mp", [(i, (i + 1) % size) for i in range(size)])
        total = total + moving
    return total


def dot(a, b, a_axis=1, b_axis=0):
    return lax.dot_general(a, b, (((a_axis,), (b_axis,)), ((), ())), preferred_element_type=F32)


def body(
    hidden_in, lengths, cotangent, qkv_weight, qv_bias, out_weight, out_bias, attn_gain,
    attn_shift, up_weight, up_bias, down_weight, down_bias, ffn_gain, ffn_shift,
):
    seqs, span, feat = hidden_in.shape
    span_dp = lax.axis_size("dp")
    own = feat // span_dp
    width = qkv_weight.shape[3]
    units = up_weight.shape[2]
    heads = width // HEAD_DIM
    keymask = jnp.arange(span)[None, :] < lengths[:, None]
    rowmask = keymask.astype(F32).reshape(-1, 1)
    hidden = hidden_in.reshape(-1, feat)

    vectors = jnp.concatenate(
        [
            v.reshape(-1, own)
            for v in (
                out_bias, attn_gain, attn_shift, down_bias, ffn_gain, ffn_shift, qv_bias, up_bias
            )
        ],
        axis=0,
    )
    used = vectors.shape[0]
    vectors = jnp.pad(vectors, ((0, 16 - used), (0, 128 - own)))
    qk_w, value_w, up_w, down_t, out_t, small = gather_all(
        (
            qkv_weight[0, :, :2].reshape(own, 2 * width),
            qkv_weight[0, :, 2],
            up_weight[0],
            down_weight[0].T,
            out_weight[0].T,
            vectors,
        )
    )
    small = small.reshape(span_dp, 16, 128)[:, :used, :own].astype(F32)
    rows = small[:, :6].transpose(1, 0, 2).reshape(6, feat)
    out_b, gain_a, shift_a, down_b, gain_f, shift_f = (rows[i : i + 1] for i in range(6))
    qv_b = small[:, 6].reshape(span_dp, 2, -1).transpose(1, 0, 2).reshape(2, width)
    up_b = small[:, 7:].reshape(1, units)

    inputs_b = hidden.astype(BF16)
    projected = dot(inputs_b, qk_w).reshape(seqs, span, 2, heads, HEAD_DIM)
    value_part = dot(inputs_b, value_w).reshape(seqs, span, heads, HEAD_DIM)
    biases = qv_b.reshape(2, heads, HEAD_DIM)
    queries = (projected[:, :, 0] + biases[0]).astype(BF16)
    keys_b = projected[:, :, 1].astype(BF16)
    values = (value_part + biases[1]).astype(BF16)
    scores = attend_scores(queries, keys_b, keymask)
    row_peak = jnp.max(scores, axis=-1, keepdims=True)
    logsum = row_peak + jnp.log(jnp.sum(jnp.exp(scores - row_peak), axis=-1, keepdims=True))
    probs_f = jnp.exp(scores - logsum)
    probs_b = probs_f.astype(BF16)
    context = jnp.einsum("bhqk,bkhe->bqhe", probs_b, values, preferred_element_type=F32)
    context = context.astype(BF16).reshape(seqs * span, width)
    attended = both_cores(dot(context, out_t, 1, 1)) + out_b
    mid, scaled_a, inverse_a = normalize(hidden + attended, gain_a, shift_a)
    mid_b = mid.astype(BF16)
    pre_act = dot(mid_b, up_w) + up_b
    act_b = gelu_exact(pre_act).astype(BF16)
    mlp_out = both_cores(dot(act_b, down_t, 1, 1)) + down_b
    output, scaled_f, inverse_f = normalize(mid + mlp_out, gain_f, shift_f)
    hidden_out = (output * rowmask).reshape(seqs, span, feat)

    upstream = cotangent.reshape(-1, feat) * rowmask
    d_resid_f, grad_gain_f, grad_shift_f = normalize_back(upstream, scaled_f, inverse_f, gain_f)
    grad_down_b = jnp.sum(d_resid_f, axis=0)
    mlp_b = d_resid_f.astype(BF16)
    grad_down = dot(mlp_b, act_b, 0, 0)
    d_pre = dot(mlp_b, down_t) * gelu_slope(pre_act)
    d_pre_b = d_pre.astype(BF16)
    grad_up = dot(mid_b, d_pre_b, 0, 0)
    grad_up_b = jnp.sum(d_pre, axis=0)
    d_mid = d_resid_f + both_cores(dot(d_pre_b, up_w, 1, 1))
    d_resid_a, grad_gain_a, grad_shift_a = normalize_back(d_mid, scaled_a, inverse_a, gain_a)
    grad_out_b = jnp.sum(d_resid_a, axis=0)
    attn_b = d_resid_a.astype(BF16)
    grad_out = dot(attn_b, context, 0, 0)
    d_context = dot(attn_b, out_t).astype(BF16).reshape(seqs, span, heads, HEAD_DIM)
    d_probs = jnp.einsum("bqhe,bkhe->bhqk", d_context, values, preferred_element_type=F32)
    d_values = jnp.einsum("bhqk,bqhe->bkhe", probs_b, d_context, preferred_element_type=F32)
    centred = jnp.sum(probs_f * d_probs, axis=-1, keepdims=True)
    d_scores = (probs_f * (d_probs - centred) * 0.125).astype(BF16)
    d_queries = jnp.einsum("bhqk,bkhe->bqhe", d_scores, keys_b, preferred_element_type=F32)
    d_keys = jnp.einsum("bhqk,bqhe->bkhe", d_scores, queries, preferred_element_type=F32)
    grad_qv = jnp.stack(
        [jnp.sum(d_queries, axis=(0, 1)).reshape(-1), jnp.sum(d_values, axis=(0, 1)).reshape(-1)]
    )
    d_qk = (
        jnp.stack([d_queries, d_keys], axis=2).astype(BF16).reshape(seqs * span, 2 * width)
    )
    d_value = d_values.astype(BF16).reshape(seqs * span, width)
    grad_qk = dot(inputs_b, d_qk, 0, 0)
    grad_value = dot(inputs_b, d_value, 0, 0)
    input_part = dot(d_qk, qk_w, 1, 1) + dot(d_value, value_w, 1, 1)
    grad_input = (d_resid_a + both_cores(input_part)).reshape(seqs, span, feat)

    grad_rows = jnp.stack(
        [grad_out_b, grad_gain_a, grad_shift_a, grad_down_b, grad_gain_f, grad_shift_f]
    )
    grad_small = jnp.concatenate(
        [
            grad_rows.reshape(6, span_dp, own).transpose(1, 0, 2),
            grad_qv.reshape(2, span_dp, -1).transpose(1, 0, 2).reshape(span_dp, 1, own),
            grad_up_b.reshape(span_dp, -1, own),
        ],
        axis=1,
    )
    grad_small = jnp.pad(grad_small, ((0, 0), (0, 16 - used), (0, 128 - own))).reshape(-1, 128)
    qk_g, value_g, up_g, down_g, out_g, small_g = scatter_all(
        tuple(g.astype(BF16) for g in (grad_qk, grad_value, grad_up, grad_down, grad_out, grad_small))
    )
    vec = [small_g[i : i + 1, :own] for i in range(6)]
    return (
        hidden_out,
        grad_input,
        jnp.concatenate([qk_g, value_g], axis=1).reshape(1, own, 3, width),
        small_g[6, :own].reshape(1, 2, -1),
        out_g.T[None],
        vec[0],
        vec[1],
        vec[2],
        up_g[None],
        small_g[7:used, :own].reshape(1, -1),
        down_g.T[None],
        vec[3],
        vec[4],
        vec[5],
    )


def solution(mesh):
    return jax.shard_map(
        body,
        mesh=mesh,
        in_specs=(
            P("dp", None, None),
            P("dp"),
            P("dp", None, None),
            P(None, "dp", None, "mp"),
            P(None, None, ("mp", "dp")),
            P(None, "mp", "dp"),
            P(None, "dp"),
            P(None, "dp"),
            P(None, "dp"),
            P(None, "dp", "mp"),
            P(None, ("mp", "dp")),
            P(None, "mp", "dp"),
            P(None, "dp"),
            P(None, "dp"),
            P(None, "dp"),
        ),
        out_specs=(
            P("dp", None, None),
            P("dp", None, None),
            P(None, "dp", None, "mp"),
            P(None, None, ("mp", "dp")),
            P(None, "mp", "dp"),
            P(None, "dp"),
            P(None, "dp"),
            P(None, "dp"),
            P(None, "dp", "mp"),
            P(None, ("mp", "dp")),
            P(None, "mp", "dp"),
            P(None, "dp"),
            P(None, "dp"),
            P(None, "dp"),
        ),
        check_vma=False,
    )
```
